32 devices in a mesh: chan: 8 (over z, x), row: 4 (over y, core).
Axes of the slice: x: 2, y: 2, z: 4, core: 2. Of those that a mesh axis runs over, the one named last changes fastest.
Arguments:
- amplitudes: bfloat16 [2048, 8, 640], P('row', 'chan'), may hold values from -6 to 6
- block_rows: int32 [8], P('chan'), may hold values from 256 to 2048, as said below
- recoupling: bfloat16 [8, 8], replicated, may hold values from -1 to 2
- interaction: bfloat16 [2048, 8, 2048], P(None, 'chan', 'row'), may hold values from -0.125 to 0.125
Outputs:
- residual: bfloat16 [2048, 8, 640], P('row', 'chan')
The draws below stay inside these ranges and needn't reach their ends.
Inputs may be any that keep to these rules, and one draw needn't show every extreme that they name: `block_rows`: each entry is at least 256 and at most 2048; some channel has exactly 2048 live rows.
All inputs are finite; a program needn't handle non-finite values.
Results may differ from the reference program's by a relative error of at most 0.015.
Values may be sent and summed in bfloat16 or wider, within the bound.
No kernel may reach another device: no remote copies, remote signals or barrier semaphores. Data moves between devices by JAX's collectives and lax.ppermute only.
A program may use at most 64 MiB of HBM per device.

```python
import math
import jax
import jax.numpy as jnp
from jax import lax

P_SIZE = 2048
Q = 640
NJ = 8
N_ROW = 4


def draw_block_rows(key, part):
    key = jax.random.fold_in(key, 11)
    first_key, second_key = jax.random.split(key)
    lengths = jax.random.randint(first_key, (NJ,), P_SIZE // 8, P_SIZE + 1, dtype=jnp.int32)
    largest_channel = jax.random.randint(second_key, (), 0, NJ, dtype=jnp.int32)
    return lengths.at[largest_channel].set(P_SIZE)


def draw_recoupling(key, part):
    key = jax.random.fold_in(key, 12)
    spread = jnp.clip(jax.random.normal(key, (NJ, NJ), jnp.float32), -4.0, 4.0) * 0.5
    matrix = jnp.eye(NJ, dtype=jnp.float32) + spread / math.sqrt(NJ)
    return matrix.astype(jnp.bfloat16)


def shard_levels(own_key, dims, pieces, least, largest):
    def one(dim, shards_of):
        draws = jax.random.uniform(jax.random.fold_in(jax.random.fold_in(own_key, 6), dim), (shards_of,), jnp.float32, least / len(pieces), largest / len(pieces))
        return jnp.repeat(jnp.exp(draws), dims[dim] // shards_of).reshape((-1,) + (1,) * (len(dims) - dim - 1))

    gain = one(*pieces[0])
    for cut in pieces[1:]:
        gain = gain * one(*cut)
    return gain


def noise(rng, shape, scale, bound, pieces=(), kind=jnp.bfloat16):
    gain = shard_levels(rng, shape, pieces, -0.22, 0.18) if pieces else 1.0
    array = jax.random.normal(rng, shape, jnp.float32) * scale * gain
    return jnp.minimum(jnp.maximum(array, -bound), bound).astype(kind)


def setup_inputs(seed: int = 0) -> dict:
    keys = jax.random.split(jax.random.key(seed), 5)
    return {
        "amplitudes": noise(keys[0], (P_SIZE, NJ, Q), 1.0, 6.0, ((0, 4), (1, 8))),
        "block_rows": draw_block_rows(jax.random.fold_in(keys[4], 71), 0),
        "recoupling": draw_recoupling(jax.random.fold_in(keys[4], 71), 0),
        "interaction": noise(keys[3], (P_SIZE, NJ, P_SIZE), P_SIZE ** -0.5, 0.125, ((1, 8), (2, 4))),
    }


def recouple(data, matrix, pattern):
    block_len = 32
    blocks = data.reshape(P_SIZE // block_len, block_len, NJ, Q)
    wide = matrix.astype(jnp.float32)

    def one_block(row_block):
        return jnp.einsum(pattern, wide, row_block.astype(jnp.float32), precision=lax.Precision.HIGHEST).astype(jnp.bfloat16)

    return lax.map(one_block, blocks).reshape(P_SIZE, NJ, Q)


def reference(amplitudes, block_rows, recoupling, interaction):
    row_identifiers = jnp.arange(P_SIZE, dtype=jnp.int32)
    live = row_identifiers[:, None] < block_rows[None, :]
    zero = jnp.zeros((), jnp.bfloat16)
    masked = jnp.where(live[:, :, None], amplitudes, zero)
    cross = recouple(masked, recoupling, "kj,rjq->rkq")
    grouped_row_list = P_SIZE // N_ROW

    def cycle_channel(chan_id):
        weights = lax.dynamic_index_in_dim(interaction, chan_id, 1, keepdims=False)
        cross_block = lax.dynamic_index_in_dim(cross, chan_id, 1, keepdims=False)
        weights = weights.reshape(P_SIZE, N_ROW, grouped_row_list).astype(jnp.float32)
        cross_block = cross_block.reshape(N_ROW, grouped_row_list, Q).astype(jnp.float32)
        partials = jnp.einsum("pkr,krq->kpq", weights, cross_block, precision=lax.Precision.HIGHEST)
        rounded = lax.optimization_barrier(partials.astype(jnp.bfloat16)).astype(jnp.float32)
        return jnp.sum(rounded, axis=0).astype(jnp.bfloat16)

    reduced_total = lax.map(cycle_channel, jnp.arange(NJ, dtype=jnp.int32))
    reduced_total = jnp.moveaxis(reduced_total, 0, 1)
    back = recouple(reduced_total, recoupling, "jk,rjq->rkq")
    return jnp.where(live[:, :, None], back, zero)
```

```python
import jax
import jax.numpy as jnp
from jax import lax
from jax.sharding import PartitionSpec as P

F32 = jnp.float32
BF16 = jnp.bfloat16


def chunk_bounds(columns, pieces):
    unit = 128 if columns % 128 == 0 else 1
    units = columns // unit
    pieces = min(pieces, units)
    marks = [units * i // pieces * unit for i in range(pieces + 1)]
    return list(zip(marks[:-1], marks[1:]))


def solution(mesh):
    n_chan, n_row = mesh.shape["chan"], mesh.shape["row"]
    chan_bits = [1 << b for b in range(n_chan.bit_length() - 1)]
    row_bits = [1 << b for b in range(n_row.bit_length() - 1)]
    gather_bits = [chan_bits[-1], chan_bits[0]]
    reduce_bits = [b for b in chan_bits if b not in gather_bits]

    def swap(x, axis, size, bit):
        return lax.ppermute(x, axis, [(i, i ^ bit) for i in range(size)])

    def on_device(amplitudes, block_rows, recoupling, interaction):
        rows_here, _, columns = amplitudes.shape
        c = lax.axis_index("chan")
        g = lax.axis_index("row")
        local_rows = g * rows_here + lax.iota(jnp.int32, rows_here)
        live = (local_rows < block_rows[0])[:, None]
        zero = jnp.zeros((), BF16)
        index = lax.iota(jnp.int32, n_chan)
        pick = ((c ^ index)[:, None] == index[None, :]).astype(BF16)
        coef = jnp.dot(
            jnp.dot(pick, recoupling, preferred_element_type=F32).astype(BF16),
            pick.T, preferred_element_type=F32)

        own = amplitudes.reshape(rows_here, columns)
        weights = interaction.reshape(interaction.shape[0], interaction.shape[2])

        def gather(block):
            held = {0: block}
            for bit in gather_bits:
                held.update({m ^ bit: swap(v, "chan", n_chan, bit) for m, v in list(held.items())})
            return held

        def mix(held, t, matrix):
            return sum(matrix[t, m] * v.astype(F32) for m, v in held.items())

        def spread_targets(bits):
            out = [0]
            for bit in bits:
                out += [t ^ bit for t in out]
            return out

        def recouple_in(block):
            held = gather(block)
            part = {t: mix(held, t, coef) for t in spread_targets(reduce_bits)}
            for bit in reversed(reduce_bits):
                keep = [t for t in part if not t & bit]
                part = {t: part[t] + swap(part[t ^ bit].astype(BF16), "chan", n_chan, bit).astype(F32) for t in keep}
            return part[0].astype(BF16)

        def recouple_out(block):
            held = {0: block}
            for bit in reduce_bits:
                held.update({m ^ bit: swap(v, "chan", n_chan, bit) for m, v in list(held.items())})
            part = {t: mix(held, t, coef.T) for t in spread_targets(gather_bits)}
            for bit in reversed(gather_bits):
                keep = [t for t in part if not t & bit]
                part = {t: part[t] + swap(part[t ^ bit].astype(BF16), "chan", n_chan, bit).astype(F32) for t in keep}
            return part[0].astype(BF16)

        def sum_rows(partial):
            part = partial.reshape(n_row, -1, partial.shape[-1])
            for bit in row_bits:
                pairs = part.reshape(part.shape[0] // 2, 2, *part.shape[1:])
                mine = (g & bit) // bit
                kept = lax.dynamic_index_in_dim(pairs, mine, 1, keepdims=False)
                sent = lax.dynamic_index_in_dim(pairs, 1 - mine, 1, keepdims=False)
                part = (kept.astype(F32) + swap(sent, "row", n_row, bit).astype(F32)).astype(BF16)
            return part[0]

        outs = []
        for lo, hi in chunk_bounds(columns, 5):
            block = jnp.where(live, own[:, lo:hi], zero)
            cross = recouple_in(block)
            partial = jnp.dot(weights, cross, preferred_element_type=F32).astype(BF16)
            outs.append(jnp.where(live, recouple_out(sum_rows(partial)), zero))
        return jnp.concatenate(outs, axis=1).reshape(amplitudes.shape)

    return jax.shard_map(
        on_device,
        mesh=mesh,
        in_specs=(P("row", "chan", None), P("chan"), P(), P(None, "chan", "row")),
        out_specs=P("row", "chan", None),
        check_vma=False,
    )
```

```python
import functools
import heapq

import jax
import jax.numpy as jnp
from jax import lax
from jax.experimental import pallas as pl
from jax.experimental.pallas import tpu as pltpu
from jax.sharding import PartitionSpec as P

F32 = jnp.float32
BF16 = jnp.bfloat16
SLAB = 64
MATMUL_ROWS = 256
VMEM_LIMIT = 16 * 1024 * 1024
PERIOD = 5.2
EARLY = 3.5
AFTER_FAR = 6.5
AFTER_CORNER = 5.5
AFTER_PARTIAL = 5.2
AFTER_CORE = 2.0
AFTER_ROW = 4.0
AFTER_LAST = 4.2

smem = pl.BlockSpec(memory_space=pltpu.SMEM)
vmem = pl.BlockSpec(memory_space=pltpu.VMEM)
unread = pl.BlockSpec(memory_space=pl.ANY)


def chunk_bounds(columns):
    width = 128 if columns % 128 == 0 else columns
    return [(lo, width) for lo in range(0, columns, width)]


class Chain:
    def __init__(self):
        self.token = []

    def call(self, kernel, name, out_shape, scalars, arrays, scratch=(), out_specs=None, whole=(), aliases=None):
        count = len(scalars) + len(arrays) + len(whole)
        tokens = len(self.token)

        def body(*refs):
            kernel(*refs[:count], *refs[count + tokens:count + tokens + len(out_shape)], *refs[count + tokens + len(out_shape) + 1:])

        *outs, token = pl.pallas_call(
            body, name=name, out_shape=[*out_shape, jax.ShapeDtypeStruct((8, 128), F32)],
            in_specs=[smem] * len(scalars) + [vmem] * len(arrays) + [unread] * (len(whole) + tokens),
            out_specs=[*(out_specs or [vmem] * len(out_shape)), unread],
            scratch_shapes=list(scratch),
            input_output_aliases=aliases or {},
            compiler_params=pltpu.CompilerParams(vmem_limit_bytes=VMEM_LIMIT),
            cost_estimate=pl.CostEstimate(flops=0, transcendentals=0, bytes_accessed=0),
        )(*scalars, *arrays, *whole, *self.token)
        self.token = [token]
        return outs

    def pin(self, *arrays):
        return self.call(
            lambda *refs: None, "pin", [like(a) for a in arrays], [], [], out_specs=[unread] * len(arrays), whole=arrays,
            aliases={i: i for i in range(len(arrays))})


def like(array):
    return jax.ShapeDtypeStruct(array.shape, array.dtype)


def slabs(rows, body, step=SLAB):
    step = step if rows % step == 0 else rows

    @pl.loop(0, rows // step)
    def _(i):
        body(pl.ds(pl.multiple_of(i * step, step), step))


def masked(total, at, left):
    row = lax.broadcasted_iota(jnp.int32, total.shape, 0) + at.start
    return jnp.where(row < left, total, 0.0).astype(BF16)


def mask_chunk(chain, place, block_rows, own, lo, width):
    rows = own.shape[0]

    def kernel(place_ref, length_ref, own_ref, out_ref):
        left = length_ref[0] - place_ref[1] * rows

        def body(at):
            out_ref[at, :] = masked(own_ref[at, lo:lo + width].astype(F32), at, left)

        slabs(rows, body)

    return chain.call(kernel, "mask_chunk", [jax.ShapeDtypeStruct((rows, width), BF16)], [place, block_rows], [own])[0]


def mixed(matrix_ref, c, held, at, target, transposed):
    total = None
    for source, ref in held:
        t, m = c ^ target, c ^ source
        weight = matrix_ref[m, t] if transposed else matrix_ref[t, m]
        term = ref[at, :].astype(F32) * weight
        total = term if total is None else total + term
    return total


def stacked(count, rows, width):
    return jax.ShapeDtypeStruct((count, rows, width), BF16)


def mix(chain, place, matrix, held, targets, received, transposed):
    rows, width = held[0][1].shape

    def kernel(place_ref, matrix_ref, *refs):
        held_refs = [(m, ref) for (m, _), ref in zip(held, refs)]
        received_refs = refs[len(held):-1]
        out_ref = refs[-1]

        def body(at):
            for i, t in enumerate(targets):
                total = mixed(matrix_ref, place_ref[0], held_refs, at, t, transposed)
                for (_, names), ref in zip(received, received_refs):
                    if t in names:
                        total = total + ref[names.index(t), at, :].astype(F32)
                out_ref[i, at, :] = total.astype(BF16)

        slabs(rows, body)

    arrays = [b for _, b in held] + [r for r, _ in received]
    return chain.call(kernel, "mix", [stacked(len(targets), rows, width)], [place, matrix], arrays)[0]


def mix_multiply(chain, place, matrix, held, received, weights, sent, kept):
    rows, width = held[0][1].shape
    group = weights.shape[0] // (len(sent) + len(kept))

    def kernel(place_ref, matrix_ref, *refs):
        held_refs = [(m, ref) for (m, _), ref in zip(held, refs)]
        received_refs = refs[len(held):len(held) + len(received)]
        weights_ref, sent_ref, kept_ref, cross_ref = refs[len(held) + len(received):]

        def body(at):
            total = mixed(matrix_ref, place_ref[0], held_refs, at, 0, False)
            for ref in received_refs:
                total = total + ref[0, at, :].astype(F32)
            cross_ref[at, :] = total.astype(BF16)

        slabs(rows, body)
        for names, out_ref in ((sent, sent_ref), (kept, kept_ref)):
            for i, d in enumerate(names):
                base = (place_ref[1] ^ d) * group

                def rows_of(at):
                    from_row = pl.ds(pl.multiple_of(base + at.start, at.size), at.size)
                    out_ref[i, at, :] = jnp.dot(
                        weights_ref[from_row, :], cross_ref[...], preferred_element_type=F32).astype(BF16)

                slabs(group, rows_of, MATMUL_ROWS)

    arrays = [b for _, b in held] + received + [weights]
    outs = [stacked(len(sent), group, width), stacked(len(kept), group, width)]
    return chain.call(kernel, "mix_multiply", outs, [place, matrix], arrays, scratch=[pltpu.VMEM((rows, width), BF16)])


def add_up(chain, stacks, targets):
    _, rows, width = stacks[0][0].shape

    def kernel(*refs):
        def body(at):
            for i, t in enumerate(targets):
                terms = [ref[names.index(t), at, :].astype(F32) for (_, names), ref in zip(stacks, refs) if t in names]
                refs[-1][i, at, :] = functools.reduce(lambda a, b: a + b, terms).astype(BF16)

        slabs(rows, body)

    return chain.call(kernel, "add_up", [stacked(len(targets), rows, width)], [], [s for s, _ in stacks])[0]


def finish(chain, place, matrix, block_rows, held, received, lo, columns, result):
    rows, width = held[0][1].shape

    def kernel(place_ref, matrix_ref, length_ref, *refs):
        left = length_ref[0] - place_ref[1] * rows
        held_refs = [(m, ref) for (m, _), ref in zip(held, refs)]
        received_refs = refs[len(held):len(held) + len(received)]
        out_ref, chunk_ref, done = refs[-3:]

        def body(at):
            total = mixed(matrix_ref, place_ref[0], held_refs, at, 0, True)
            for ref in received_refs:
                total = total + ref[0, at, :].astype(F32)
            chunk_ref[at, :] = masked(total, at, left)

        slabs(rows, body)
        copy = pltpu.make_async_copy(chunk_ref, out_ref.at[:, lo:lo + width], done)
        copy.start()
        copy.wait()

    arrays = [b for _, b in held] + received
    whole = [] if result is None else [result]
    return chain.call(
        kernel, "finish", [jax.ShapeDtypeStruct((rows, columns), BF16)], [place, matrix, block_rows], arrays,
        scratch=[pltpu.VMEM((rows, width), BF16), pltpu.SemaphoreType.DMA(())], out_specs=[unread],
        whole=whole, aliases={3 + len(arrays): 0} if whole else {})[0]


def solution(mesh):
    n_chan, n_row = mesh.shape["chan"], mesh.shape["row"]
    chan_bits = [1 << b for b in range(n_chan.bit_length() - 1)]
    row_bits = [1 << b for b in range(n_row.bit_length() - 1)]
    far, near = chan_bits[-1], chan_bits[0]
    reduce_bits = [b for b in reversed(chan_bits) if b not in (far, near)]

    def swap(x, axis, size, bit):
        return lax.ppermute(x, axis, [(i, i ^ bit) for i in range(size)])

    def on_device(amplitudes, block_rows, recoupling, interaction):
        rows, _, columns = amplitudes.shape
        place = jnp.stack([lax.axis_index("chan"), lax.axis_index("row")]).astype(jnp.int32)
        matrix = recoupling.astype(F32)
        own = amplitudes.reshape(rows, columns)
        weights = interaction.reshape(interaction.shape[0], interaction.shape[2])
        chain = Chain()
        result = None

        def recouple(block, transposed, last, after_partial):
            other = swap(block, "chan", n_chan, far)
            beside = swap(block, "chan", n_chan, near)
            yield AFTER_FAR
            other, beside = chain.pin(other, beside)
            corner = swap(other, "chan", n_chan, near)
            held = [(0, block), (far, other), (near, beside), (far ^ near, corner)]
            targets = [0]
            for bit in reduce_bits:
                targets = targets + [t ^ bit for t in targets]
            received = []
            yield AFTER_CORNER
            for bit in reduce_bits:
                sent = [t for t in targets if t & bit]
                targets = [t for t in targets if not t & bit]
                part = mix(chain, place, matrix, held, sent, received, transposed)
                received.append((swap(part, "chan", n_chan, bit), [t ^ bit for t in sent]))
                yield after_partial
            return last(held, [r for r, _ in received])

        def one_chunk(lo, width):
            block = mask_chunk(chain, place, block_rows, own, lo, width)
            bit = row_bits[0]
            sent = [d for d in range(n_row) if d & bit]
            targets = [d for d in range(n_row) if not d & bit]
            parts, kept = yield from recouple(
                block, False,
                lambda held, received: mix_multiply(chain, place, matrix, held, received, weights, sent, targets),
                AFTER_PARTIAL)
            stacks = [(kept, targets), (swap(parts, "row", n_row, bit), targets)]
            yield AFTER_CORE
            for bit in row_bits[1:]:
                sent = [d for d in targets if d & bit]
                targets = [d for d in targets if not d & bit]
                stacks.append((swap(add_up(chain, stacks, sent), "row", n_row, bit), targets))
                yield AFTER_ROW
            block = add_up(chain, stacks, targets)[0]

            def last(held, received):
                nonlocal result
                result = finish(chain, place, matrix, block_rows, held, received, lo, columns, result)

            yield from recouple(block, True, last, AFTER_LAST)

        queue = [(i * PERIOD - (EARLY if i else 0), i, one_chunk(lo, width)) for i, (lo, width) in enumerate(chunk_bounds(columns))]
        while queue:
            time, i, work = heapq.heappop(queue)
            wait = next(work, None)
            if wait is not None:
                heapq.heappush(queue, (max(time, i * PERIOD) + wait, i, work))
        return result.reshape(amplitudes.shape)

    return jax.shard_map(
        on_device,
        mesh=mesh,
        in_specs=(P("row", "chan", None), P("chan"), P(), P(None, "chan", "row")),
        out_specs=P("row", "chan", None),
        check_vma=False,
    )
```

```python
import functools

import jax
import jax.numpy as jnp
from jax import lax
from jax.experimental import pallas as pl
from jax.experimental.pallas import tpu as pltpu
from jax.sharding import PartitionSpec as P

F32 = jnp.float32
BF16 = jnp.bfloat16
SLAB = 64
MATMUL_ROWS = 256
VMEM_LIMIT = 16 * 1024 * 1024
smem = pl.BlockSpec(memory_space=pltpu.SMEM)
vmem = pl.BlockSpec(memory_space=pltpu.VMEM)
unread = pl.BlockSpec(memory_space=pl.ANY)


def chunk_bounds(columns):
    width = 128 if columns % 128 == 0 else columns
    return [(lo, width) for lo in range(0, columns, width)]


def call(kernel, name, out_shape, arrays, scalars=(), scratch=(), out_specs=None, whole=(), after=(), aliases=None):
    count = len(scalars) + len(arrays) + len(whole)

    def body(*refs):
        kernel(*refs[:count], *refs[count + len(after):])

    return pl.pallas_call(
        body, name=name, out_shape=list(out_shape),
        in_specs=[smem] * len(scalars) + [vmem] * len(arrays) + [unread] * (len(whole) + len(after)),
        out_specs=out_specs or [vmem] * len(out_shape),
        scratch_shapes=list(scratch),
        input_output_aliases=aliases or {},
        compiler_params=pltpu.CompilerParams(vmem_limit_bytes=VMEM_LIMIT),
        cost_estimate=pl.CostEstimate(flops=0, transcendentals=0, bytes_accessed=0),
    )(*scalars, *arrays, *whole, *after)


def like(array):
    return jax.ShapeDtypeStruct(array.shape, array.dtype)


def slabs(rows, body, step=SLAB):
    step = step if rows % step == 0 else rows

    @pl.loop(0, rows // step)
    def _(i):
        body(pl.ds(pl.multiple_of(i * step, step), step))


def masked(total, at, left):
    row = lax.broadcasted_iota(jnp.int32, total.shape, 0) + at.start
    return jnp.where(row < left, total, 0.0).astype(BF16)


def stacked(count, rows, width):
    return jax.ShapeDtypeStruct((count, rows, width), BF16)


def mask_first(block_rows, own, lo, width):
    rows = own.shape[0]

    def kernel(length_ref, own_ref, out_ref, left_ref):
        left = length_ref[0] - lax.axis_index("row") * rows
        left_ref[...] = jnp.full(left_ref.shape, left, jnp.int32)

        def body(at):
            out_ref[at, :] = masked(own_ref[at, lo:lo + width].astype(F32), at, left)

        slabs(rows, body)

    outs = [jax.ShapeDtypeStruct((rows, width), BF16), jax.ShapeDtypeStruct((8, width), jnp.int32)]
    return call(kernel, "mask_first", outs, [own], [block_rows])


def mask_chunk(left, own, lo, width, after):
    rows = own.shape[0]

    def kernel(left_ref, own_ref, out_ref):
        def body(at):
            out_ref[at, :] = masked(own_ref[at, lo:lo + width].astype(F32), at, left_ref[0:1, :])

        slabs(rows, body)

    return call(kernel, "mask_chunk", [jax.ShapeDtypeStruct((rows, width), BF16)], [left, own], after=after)[0]


def coefficients(matrix, n_chan, entries, width):
    count = -(-len(entries) // 8) * 8

    def kernel(matrix_ref, table_ref):
        c = lax.axis_index("chan")
        for i, (t, m) in enumerate(entries):
            table_ref[i:i + 1, :] = jnp.full((1, width), matrix_ref[c ^ t, c ^ m], F32)

    return call(kernel, "coefficients", [jax.ShapeDtypeStruct((count, width), F32)], [], [matrix])[0]


def mixed(table_ref, entries, held, at, target):
    total = None
    for source, ref in held:
        entry = entries.index((target, source))
        term = ref[at, :].astype(F32) * table_ref[entry:entry + 1, :]
        total = term if total is None else total + term
    return total


def mix(table, entries, held, targets, received):
    rows, width = held[0][1].shape

    def kernel(table_ref, *refs):
        held_refs = [(m, ref) for (m, _), ref in zip(held, refs)]
        received_refs = refs[len(held):-1]
        out_ref = refs[-1]

        def body(at):
            for i, t in enumerate(targets):
                total = mixed(table_ref, entries, held_refs, at, t)
                for (_, names), ref in zip(received, received_refs):
                    if t in names:
                        total = total + ref[names.index(t), at, :].astype(F32)
                out_ref[i, at, :] = total.astype(BF16)

        slabs(rows, body)

    arrays = [table] + [b for _, b in held] + [r for r, _ in received]
    return call(kernel, "mix", [stacked(len(targets), rows, width)], arrays)[0]


def mix_multiply(table, entries, held, received, weights, sent, kept):
    rows, width = held[0][1].shape
    group = weights.shape[0] // (len(sent) + len(kept))

    def kernel(table_ref, *refs):
        held_refs = [(m, ref) for (m, _), ref in zip(held, refs)]
        received_refs = refs[len(held):len(held) + len(received)]
        weights_ref, sent_ref, kept_ref, cross_ref = refs[len(held) + len(received):]
        g = lax.axis_index("row")

        def body(at):
            total = mixed(table_ref, entries, held_refs, at, 0)
            for ref in received_refs:
                total = total + ref[0, at, :].astype(F32)
            cross_ref[at, :] = total.astype(BF16)

        slabs(rows, body)
        for names, out_ref in ((sent, sent_ref), (kept, kept_ref)):
            for i, d in enumerate(names):
                base = (g ^ d) * group

                def rows_of(at):
                    from_row = pl.ds(pl.multiple_of(base + at.start, at.size), at.size)
                    out_ref[i, at, :] = jnp.dot(
                        weights_ref[from_row, :], cross_ref[...], preferred_element_type=F32).astype(BF16)

                slabs(group, rows_of, MATMUL_ROWS)

    arrays = [table] + [b for _, b in held] + received + [weights]
    outs = [stacked(len(sent), group, width), stacked(len(kept), group, width)]
    return call(kernel, "mix_multiply", outs, arrays, scratch=[pltpu.VMEM((rows, width), BF16)])


def add_up(stacks, targets):
    _, rows, width = stacks[0][0].shape

    def kernel(*refs):
        def body(at):
            for i, t in enumerate(targets):
                terms = [ref[names.index(t), at, :].astype(F32) for (_, names), ref in zip(stacks, refs) if t in names]
                refs[-1][i, at, :] = functools.reduce(lambda a, b: a + b, terms).astype(BF16)

        slabs(rows, body)

    return call(kernel, "add_up", [stacked(len(targets), rows, width)], [s for s, _ in stacks])[0]


def finish(table, entries, left, held, received, lo, columns, result):
    rows, width = held[0][1].shape

    def kernel(table_ref, left_ref, *refs):
        held_refs = [(m, ref) for (m, _), ref in zip(held, refs)]
        received_refs = refs[len(held):len(held) + len(received)]
        out_ref, chunk_ref, done = refs[-3:]

        def body(at):
            total = mixed(table_ref, entries, held_refs, at, 0)
            for ref in received_refs:
                total = total + ref[0, at, :].astype(F32)
            chunk_ref[at, :] = masked(total, at, left_ref[0:1, :])

        slabs(rows, body)
        copy = pltpu.make_async_copy(chunk_ref, out_ref.at[:, lo:lo + width], done)
        copy.start()
        copy.wait()

    arrays = [table, left] + [b for _, b in held] + received
    whole = [] if result is None else [result]
    return call(
        kernel, "finish", [jax.ShapeDtypeStruct((rows, columns), BF16)], arrays,
        scratch=[pltpu.VMEM((rows, width), BF16), pltpu.SemaphoreType.DMA(())], out_specs=[unread],
        whole=whole, aliases={len(arrays): 0} if whole else {})[0]


def solution(mesh):
    n_chan, n_row = mesh.shape["chan"], mesh.shape["row"]
    chan_bits = [1 << b for b in range(n_chan.bit_length() - 1)]
    row_bits = [1 << b for b in range(n_row.bit_length() - 1)]
    far, near = chan_bits[-1], chan_bits[0]
    reduce_bits = [b for b in reversed(chan_bits) if b not in (far, near)]

    def swap(x, axis, size, bit):
        return lax.ppermute(x, axis, [(i, i ^ bit) for i in range(size)])

    def span(bits):
        targets = [0]
        for bit in bits:
            targets = targets + [t ^ bit for t in targets]
        return targets

    def split(targets, bit):
        return [t for t in targets if t & bit], [t for t in targets if not t & bit]

    def gather(block):
        other = swap(block, "chan", n_chan, far)
        beside = swap(block, "chan", n_chan, near)
        corner = swap(other, "chan", n_chan, near)
        return [(0, block), (far, other), (near, beside), (far ^ near, corner)]

    def exchange_partials(table, entries, held):
        targets, received = span(reduce_bits), []
        for bit in reduce_bits:
            sent, targets = split(targets, bit)
            part = mix(table, entries, held, sent, received)
            received.append((swap(part, "chan", n_chan, bit), [t ^ bit for t in sent]))
        return [r for r, _ in received]

    def sum_rows(multiply):
        sent, targets = split(list(range(n_row)), row_bits[0])
        parts, kept = multiply(sent, targets)
        stacks = [(kept, targets), (swap(parts, "row", n_row, row_bits[0]), targets)]
        for bit in row_bits[1:]:
            sent, targets = split(targets, bit)
            stacks.append((swap(add_up(stacks, sent), "row", n_row, bit), targets))
        return add_up(stacks, targets)[0]

    def on_device(amplitudes, block_rows, recoupling, interaction):
        rows, _, columns = amplitudes.shape
        own = amplitudes.reshape(rows, columns)
        weights = interaction.reshape(interaction.shape[0], interaction.shape[2])
        bounds = chunk_bounds(columns)
        width = bounds[0][1]
        entries = [(t, m) for t in span(reduce_bits) for m in (0, far, near, far ^ near)]
        matrix = recoupling.astype(F32)
        table_in = coefficients(matrix, n_chan, entries, width)
        table_out = coefficients(matrix.T, n_chan, entries, width)

        first, left = mask_first(block_rows, own, *bounds[0])
        gathered = [gather(first)]
        for i, bound in enumerate(bounds[1:], 1):
            after = [gathered[0][2][1]] if i == 1 else [gathered[i - 2][1][1]]
            gathered.append(gather(mask_chunk(left, own, *bound, after)))
        result = None
        for (lo, _), held in zip(bounds, gathered):
            received = exchange_partials(table_in, entries, held)
            summed = sum_rows(lambda sent, kept: mix_multiply(table_in, entries, held, received, weights, sent, kept))
            held = gather(summed)
            received = exchange_partials(table_out, entries, held)
            result = finish(table_out, entries, left, held, received, lo, columns, result)
        return result.reshape(amplitudes.shape)

    return jax.shard_map(
        on_device,
        mesh=mesh,
        in_specs=(P("row", "chan", None), P("chan"), P(), P(None, "chan", "row")),
        out_specs=P("row", "chan", None),
        check_vma=False,
    )
```

```python
import functools
import heapq

import jax
import jax.numpy as jnp
from jax import lax
from jax.experimental import pallas as pl
from jax.experimental.pallas import tpu as pltpu
from jax.sharding import PartitionSpec as P

F32 = jnp.float32
BF16 = jnp.bfloat16
SLAB = 64
MATMUL_ROWS = 256
VMEM_LIMIT = 16 * 1024 * 1024
LINK_SHARE = {"far": 0.041, "near": 0.0205, "partial": 0.0205, "core": 0.012, "row": 0.0205}
LATENCY = 1.5

smem = pl.BlockSpec(memory_space=pltpu.SMEM)
vmem = pl.BlockSpec(memory_space=pltpu.VMEM)
unread = pl.BlockSpec(memory_space=pl.ANY)


def chunk_bounds(columns):
    if columns % 128:
        return [(0, columns)]
    marks = list(range(0, columns, 256))
    return [(lo, min(256, columns - lo)) for lo in marks]


class Chain:
    def __init__(self):
        self.token = []

    def call(self, kernel, name, out_shape, arrays, scalars=(), scratch=(), out_specs=None, whole=(), after=(), aliases=None):
        count = len(scalars) + len(arrays) + len(whole)
        outs = count + len(after) + len(self.token)

        def body(*refs):
            kernel(*refs[:count], *refs[outs:outs + len(out_shape)], *refs[outs + len(out_shape) + 1:])

        *results, token = pl.pallas_call(
            body, name=name, out_shape=[*out_shape, jax.ShapeDtypeStruct((8, 128), F32)],
            in_specs=[smem] * len(scalars) + [vmem] * len(arrays) + [unread] * (outs - len(scalars) - len(arrays)),
            out_specs=[*(out_specs or [vmem] * len(out_shape)), unread],
            scratch_shapes=list(scratch),
            input_output_aliases=aliases or {},
            compiler_params=pltpu.CompilerParams(vmem_limit_bytes=VMEM_LIMIT),
            cost_estimate=pl.CostEstimate(flops=0, transcendentals=0, bytes_accessed=0),
        )(*scalars, *arrays, *whole, *after, *self.token)
        self.token = [token]
        return results

    def pin(self, *arrays):
        return self.call(
            lambda *refs: None, "pin", [like(a) for a in arrays], [], out_specs=[unread] * len(arrays), whole=arrays,
            aliases={i: i for i in range(len(arrays))})


def like(array):
    return jax.ShapeDtypeStruct(array.shape, array.dtype)


def slabs(rows, body, step=SLAB):
    step = step if rows % step == 0 else rows

    @pl.loop(0, rows // step)
    def _(i):
        body(pl.ds(pl.multiple_of(i * step, step), step))


def masked(total, at, left):
    row = lax.broadcasted_iota(jnp.int32, total.shape, 0) + at.start
    return jnp.where(row < left, total, 0.0).astype(BF16)


def stacked(count, rows, width):
    return jax.ShapeDtypeStruct((count, rows, width), BF16)


def mask_first(chain, block_rows, own, lo, width):
    rows = own.shape[0]

    def kernel(length_ref, own_ref, out_ref, left_ref):
        left = length_ref[0] - lax.axis_index("row") * rows
        left_ref[...] = jnp.full(left_ref.shape, left, jnp.int32)

        def body(at):
            out_ref[at, :] = masked(own_ref[at, lo:lo + width].astype(F32), at, left)

        slabs(rows, body)

    outs = [jax.ShapeDtypeStruct((rows, width), BF16), jax.ShapeDtypeStruct((8, width), jnp.int32)]
    return chain.call(kernel, "mask_first", outs, [own], [block_rows])


def mask_chunk(chain, left, own, lo, width, after):
    rows = own.shape[0]

    def kernel(left_ref, own_ref, out_ref):
        def body(at):
            out_ref[at, :] = masked(own_ref[at, lo:lo + width].astype(F32), at, left_ref[0:1, :width])

        slabs(rows, body)

    return chain.call(kernel, "mask_chunk", [jax.ShapeDtypeStruct((rows, width), BF16)], [left, own], after=after)[0]


def coefficients(chain, matrix, n_chan, entries, width):
    count = -(-len(entries) // 8) * 8

    def kernel(matrix_ref, table_ref):
        c = lax.axis_index("chan")
        for i, (t, m) in enumerate(entries):
            table_ref[i:i + 1, :] = jnp.full((1, width), matrix_ref[c ^ t, c ^ m], F32)

    return chain.call(kernel, "coefficients", [jax.ShapeDtypeStruct((count, width), F32)], [], [matrix])[0]


def mixed(table_ref, entries, held, at, target):
    total = None
    for source, ref in held:
        entry = entries.index((target, source))
        term = ref[at, :].astype(F32) * table_ref[entry:entry + 1, :ref.shape[1]]
        total = term if total is None else total + term
    return total


def mix(chain, table, entries, held, targets, received):
    rows, width = held[0][1].shape

    def kernel(table_ref, *refs):
        held_refs = [(m, ref) for (m, _), ref in zip(held, refs)]
        received_refs = refs[len(held):-1]
        out_ref = refs[-1]

        def body(at):
            for i, t in enumerate(targets):
                total = mixed(table_ref, entries, held_refs, at, t)
                for (_, names), ref in zip(received, received_refs):
                    if t in names:
                        total = total + ref[names.index(t), at, :].astype(F32)
                out_ref[i, at, :] = total.astype(BF16)

        slabs(rows, body)

    arrays = [table] + [b for _, b in held] + [r for r, _ in received]
    return chain.call(kernel, "mix", [stacked(len(targets), rows, width)], arrays)[0]


def mix_multiply(chain, table, entries, held, received, weights, n_row):
    rows, width = held[0][1].shape
    group = weights.shape[0] // n_row

    def kernel(table_ref, *refs):
        held_refs = [(m, ref) for (m, _), ref in zip(held, refs)]
        received_refs = refs[len(held):len(held) + len(received)]
        weights_ref, *out_refs, cross_ref = refs[len(held) + len(received):]
        g = lax.axis_index("row")

        def body(at):
            total = mixed(table_ref, entries, held_refs, at, 0)
            for ref in received_refs:
                total = total + ref[0, at, :].astype(F32)
            cross_ref[at, :] = total.astype(BF16)

        slabs(rows, body)
        for d, out_ref in enumerate(out_refs):
            base = (g ^ d) * group

            def rows_of(at):
                from_row = pl.ds(pl.multiple_of(base + at.start, at.size), at.size)
                out_ref[at, :] = jnp.dot(weights_ref[from_row, :], cross_ref[...], preferred_element_type=F32).astype(BF16)

            slabs(group, rows_of, MATMUL_ROWS)

    arrays = [table] + [b for _, b in held] + received + [weights]
    outs = [jax.ShapeDtypeStruct((group, width), BF16)] * n_row
    return chain.call(kernel, "mix_multiply", outs, arrays, scratch=[pltpu.VMEM((rows, width), BF16)])


def add_up(chain, blocks):
    def kernel(*refs):
        def body(at):
            terms = [ref[at, :].astype(F32) for ref in refs[:-1]]
            refs[-1][at, :] = functools.reduce(lambda a, b: a + b, terms).astype(BF16)

        slabs(blocks[0].shape[0], body)

    return chain.call(kernel, "add_up", [like(blocks[0])], blocks)[0]


def finish(chain, table, entries, left, held, received, lo, columns, result):
    rows, width = held[0][1].shape

    def kernel(table_ref, left_ref, *refs):
        held_refs = [(m, ref) for (m, _), ref in zip(held, refs)]
        received_refs = refs[len(held):len(held) + len(received)]
        out_ref, chunk_ref, done = refs[-3:]

        def body(at):
            total = mixed(table_ref, entries, held_refs, at, 0)
            for ref in received_refs:
                total = total + ref[0, at, :].astype(F32)
            chunk_ref[at, :] = masked(total, at, left_ref[0:1, :width])

        slabs(rows, body)
        copy = pltpu.make_async_copy(chunk_ref, out_ref.at[:, lo:lo + width], done)
        copy.start()
        copy.wait()

    arrays = [table, left] + [b for _, b in held] + received
    whole = [] if result is None else [result]
    return chain.call(
        kernel, "finish", [jax.ShapeDtypeStruct((rows, columns), BF16)], arrays,
        scratch=[pltpu.VMEM((rows, width), BF16), pltpu.SemaphoreType.DMA(())], out_specs=[unread],
        whole=whole, aliases={len(arrays): 0} if whole else {})[0]


def solution(mesh):
    n_chan, n_row = mesh.shape["chan"], mesh.shape["row"]
    chan_bits = [1 << b for b in range(n_chan.bit_length() - 1)]
    row_bits = [1 << b for b in range(n_row.bit_length() - 1)]
    far, near = chan_bits[-1], chan_bits[0]
    reduce_bits = [b for b in reversed(chan_bits) if b not in (far, near)]

    def swap(x, axis, size, bit):
        return lax.ppermute(x, axis, [(i, i ^ bit) for i in range(size)])

    def span(bits):
        targets = [0]
        for bit in bits:
            targets = targets + [t ^ bit for t in targets]
        return targets

    def split(targets, bit):
        return [t for t in targets if t & bit], [t for t in targets if not t & bit]

    def on_device(amplitudes, block_rows, recoupling, interaction):
        rows, _, columns = amplitudes.shape
        own = amplitudes.reshape(rows, columns)
        weights = interaction.reshape(interaction.shape[0], interaction.shape[2])
        bounds = chunk_bounds(columns)
        lanes = max(width for _, width in bounds)
        entries = [(t, m) for t in span(reduce_bits) for m in (0, far, near, far ^ near)]
        matrix = recoupling.astype(F32)
        chain = Chain()
        tables, result, left, last_far = {}, None, None, None

        def table(transposed):
            if transposed not in tables:
                tables[transposed] = coefficients(chain, matrix.T if transposed else matrix, n_chan, entries, lanes)
            return tables[transposed]

        def mixing(block, transposed, note_far=None):
            other = swap(block, "chan", n_chan, far)
            beside = swap(block, "chan", n_chan, near)
            if note_far:
                note_far(other)
            yield "far"
            other, beside = chain.pin(other, beside)
            corner = swap(other, "chan", n_chan, near)
            held = [(0, block), (far, other), (near, beside), (far ^ near, corner)]
            targets, received = span(reduce_bits), []
            yield "near"
            for bit in reduce_bits:
                sent, targets = split(targets, bit)
                part = mix(chain, table(transposed), entries, held, sent, received)
                received.append((swap(part, "chan", n_chan, bit), [t ^ bit for t in sent]))
                yield "partial"
            return held, [r for r, _ in received]

        def one_chunk(lo, width):
            nonlocal result, left, last_far

            def note_far(array):
                nonlocal last_far
                last_far = array

            if left is None:
                block, left = mask_first(chain, block_rows, own, lo, width)
            else:
                block = mask_chunk(chain, left, own, lo, width, [last_far])
            held, received = yield from mixing(block, False, note_far)
            parts = mix_multiply(chain, table(False), entries, held, received, weights, n_row)
            terms, targets = {d: [part] for d, part in enumerate(parts)}, list(range(n_row))
            for bit in row_bits:
                sent, targets = split(targets, bit)
                for t in sent:
                    block = terms[t][0] if len(terms[t]) == 1 else add_up(chain, terms[t])
                    terms[t ^ bit].append(swap(block, "row", n_row, bit))
                yield "core" if bit == row_bits[0] else "row"
            block = add_up(chain, terms[0])
            held, received = yield from mixing(block, True)
            result = finish(chain, table(True), entries, left, held, received, lo, columns, result)

        free = dict.fromkeys(LINK_SHARE, 0.0)
        queue, start = [], 0.0
        for i, (lo, width) in enumerate(bounds):
            queue.append((start, i, one_chunk(lo, width)))
            start += LINK_SHARE["far"] * width
        while queue:
            time, i, work = heapq.heappop(queue)
            kind = next(work, None)
            if kind is not None:
                free[kind] = max(time, free[kind]) + LINK_SHARE[kind] * bounds[i][1]
                heapq.heappush(queue, (free[kind] + LATENCY, i, work))
        return result.reshape(amplitudes.shape)

    return jax.shard_map(
        on_device,
        mesh=mesh,
        in_specs=(P("row", "chan", None), P("chan"), P(), P(None, "chan", "row")),
        out_specs=P("row", "chan", None),
        check_vma=False,
    )
```

```python
import functools
import heapq

import jax
import jax.numpy as jnp
from jax import lax
from jax.experimental import pallas as pl
from jax.experimental.pallas import tpu as pltpu
from jax.sharding import PartitionSpec as P

F32 = jnp.float32
BF16 = jnp.bfloat16
SLAB = 64
MATMUL_ROWS = 256
VMEM_LIMIT = 16 * 1024 * 1024
LINK_SHARE = {'far': 0.0312, 'near': 0.0282, 'partial': 0.0371, 'core': 0.0223, 'row': 0.0375}
LATENCY = 1.156

smem = pl.BlockSpec(memory_space=pltpu.SMEM)
vmem = pl.BlockSpec(memory_space=pltpu.VMEM)
unread = pl.BlockSpec(memory_space=pl.ANY)


def chunk_bounds(columns):
    if columns % 128:
        return [(0, columns)]
    units = columns // 128
    units = [2] + [1] * (units - 2) if units > 2 else [units]
    out, lo = [], 0
    for unit in units:
        out.append((lo, 128 * unit))
        lo += 128 * unit
    return out


class Chain:
    def call(self, kernel, name, out_shape, arrays, scalars=(), scratch=(), out_specs=None, whole=(), after=(), aliases=None):
        count = len(scalars) + len(arrays) + len(whole)
        outs = count + len(after)

        def body(*refs):
            kernel(*refs[:count], *refs[outs:outs + len(out_shape)], *refs[outs + len(out_shape):])

        return pl.pallas_call(
            body, name=name, out_shape=list(out_shape),
            in_specs=[smem] * len(scalars) + [vmem] * len(arrays) + [unread] * (outs - len(scalars) - len(arrays)),
            out_specs=out_specs or [vmem] * len(out_shape),
            scratch_shapes=list(scratch),
            input_output_aliases=aliases or {},
            compiler_params=pltpu.CompilerParams(vmem_limit_bytes=VMEM_LIMIT),
            cost_estimate=pl.CostEstimate(flops=0, transcendentals=0, bytes_accessed=0),
        )(*scalars, *arrays, *whole, *after)

    def pin(self, *arrays):
        return self.call(
            lambda *refs: None, "pin", [like(a) for a in arrays], [], out_specs=[unread] * len(arrays), whole=arrays,
            aliases={i: i for i in range(len(arrays))})


def like(array):
    return jax.ShapeDtypeStruct(array.shape, array.dtype)


def slabs(rows, body, step=SLAB):
    step = step if rows % step == 0 else rows

    @pl.loop(0, rows // step)
    def _(i):
        body(pl.ds(pl.multiple_of(i * step, step), step))


def masked(total, at, left):
    row = lax.broadcasted_iota(jnp.int32, total.shape, 0) + at.start
    return jnp.where(row < left, total, 0.0).astype(BF16)


def stacked(count, rows, width):
    return jax.ShapeDtypeStruct((count, rows, width), BF16)


def mask_first(chain, block_rows, own, lo, width):
    rows = own.shape[0]

    def kernel(length_ref, own_ref, out_ref, left_ref):
        left = length_ref[0] - lax.axis_index("row") * rows
        left_ref[...] = jnp.full(left_ref.shape, left, jnp.int32)

        def body(at):
            out_ref[at, :] = masked(own_ref[at, lo:lo + width].astype(F32), at, left)

        slabs(rows, body)

    outs = [jax.ShapeDtypeStruct((rows, width), BF16), jax.ShapeDtypeStruct((8, 256), jnp.int32)]
    return chain.call(kernel, "mask_first", outs, [own], [block_rows])


def mask_chunk(chain, left, own, lo, width, after):
    rows = own.shape[0]

    def kernel(left_ref, own_ref, out_ref):
        def body(at):
            out_ref[at, :] = masked(own_ref[at, lo:lo + width].astype(F32), at, left_ref[0:1, :width])

        slabs(rows, body)

    return chain.call(kernel, "mask_chunk", [jax.ShapeDtypeStruct((rows, width), BF16)], [left, own], after=after)[0]


def coefficients(chain, matrix, n_chan, entries, width):
    count = -(-len(entries) // 8) * 8

    def kernel(matrix_ref, table_ref):
        c = lax.axis_index("chan")
        for i, (t, m) in enumerate(entries):
            table_ref[i:i + 1, :] = jnp.full((1, width), matrix_ref[c ^ t, c ^ m], F32)

    return chain.call(kernel, "coefficients", [jax.ShapeDtypeStruct((count, width), F32)], [], [matrix])[0]


def mixed(table_ref, entries, held, at, target):
    total = None
    for source, ref in held:
        entry = entries.index((target, source))
        term = ref[at, :].astype(F32) * table_ref[entry:entry + 1, :ref.shape[1]]
        total = term if total is None else total + term
    return total


def mix(chain, table, entries, held, targets, received):
    rows, width = held[0][1].shape

    def kernel(table_ref, *refs):
        held_refs = [(m, ref) for (m, _), ref in zip(held, refs)]
        received_refs = refs[len(held):-1]
        out_ref = refs[-1]

        def body(at):
            for i, t in enumerate(targets):
                total = mixed(table_ref, entries, held_refs, at, t)
                for (_, names), ref in zip(received, received_refs):
                    if t in names:
                        total = total + ref[names.index(t), at, :].astype(F32)
                out_ref[i, at, :] = total.astype(BF16)

        slabs(rows, body)

    arrays = [table] + [b for _, b in held] + [r for r, _ in received]
    return chain.call(kernel, "mix", [stacked(len(targets), rows, width)], arrays)[0]


def mix_multiply(chain, table, entries, held, received, weights, n_row):
    rows, width = held[0][1].shape
    group = weights.shape[0] // n_row

    def kernel(table_ref, *refs):
        held_refs = [(m, ref) for (m, _), ref in zip(held, refs)]
        received_refs = refs[len(held):len(held) + len(received)]
        weights_ref, *out_refs, cross_ref = refs[len(held) + len(received):]
        g = lax.axis_index("row")

        def body(at):
            total = mixed(table_ref, entries, held_refs, at, 0)
            for ref in received_refs:
                total = total + ref[0, at, :].astype(F32)
            cross_ref[at, :] = total.astype(BF16)

        slabs(rows, body)
        for d, out_ref in enumerate(out_refs):
            base = (g ^ d) * group

            def rows_of(at):
                from_row = pl.ds(pl.multiple_of(base + at.start, at.size), at.size)
                out_ref[at, :] = jnp.dot(weights_ref[from_row, :], cross_ref[...], preferred_element_type=F32).astype(BF16)

            slabs(group, rows_of, MATMUL_ROWS)

    arrays = [table] + [b for _, b in held] + received + [weights]
    outs = [jax.ShapeDtypeStruct((group, width), BF16)] * n_row
    return chain.call(kernel, "mix_multiply", outs, arrays, scratch=[pltpu.VMEM((rows, width), BF16)])


def add_up(chain, blocks):
    def kernel(*refs):
        def body(at):
            terms = [ref[at, :].astype(F32) for ref in refs[:-1]]
            refs[-1][at, :] = functools.reduce(lambda a, b: a + b, terms).astype(BF16)

        slabs(blocks[0].shape[0], body)

    return chain.call(kernel, "add_up", [like(blocks[0])], blocks)[0]


def finish(chain, table, entries, left, held, received, lo, columns, result):
    rows, width = held[0][1].shape

    def kernel(table_ref, left_ref, *refs):
        held_refs = [(m, ref) for (m, _), ref in zip(held, refs)]
        received_refs = refs[len(held):len(held) + len(received)]
        out_ref, chunk_ref, done = refs[-3:]

        def body(at):
            total = mixed(table_ref, entries, held_refs, at, 0)
            for ref in received_refs:
                total = total + ref[0, at, :].astype(F32)
            chunk_ref[at, :] = masked(total, at, left_ref[0:1, :width])

        slabs(rows, body)
        copy = pltpu.make_async_copy(chunk_ref, out_ref.at[:, lo:lo + width], done)
        copy.start()
        copy.wait()

    arrays = [table, left] + [b for _, b in held] + received
    whole = [] if result is None else [result]
    return chain.call(
        kernel, "finish", [jax.ShapeDtypeStruct((rows, columns), BF16)], arrays,
        scratch=[pltpu.VMEM((rows, width), BF16), pltpu.SemaphoreType.DMA(())], out_specs=[unread],
        whole=whole, aliases={len(arrays): 0} if whole else {})[0]


def solution(mesh):
    n_chan, n_row = mesh.shape["chan"], mesh.shape["row"]
    chan_bits = [1 << b for b in range(n_chan.bit_length() - 1)]
    row_bits = [1 << b for b in range(n_row.bit_length() - 1)]
    far, near = chan_bits[-1], chan_bits[0]
    reduce_bits = [b for b in reversed(chan_bits) if b not in (far, near)]

    def swap(x, axis, size, bit):
        return lax.ppermute(x, axis, [(i, i ^ bit) for i in range(size)])

    def span(bits):
        targets = [0]
        for bit in bits:
            targets = targets + [t ^ bit for t in targets]
        return targets

    def split(targets, bit):
        return [t for t in targets if t & bit], [t for t in targets if not t & bit]

    def on_device(amplitudes, block_rows, recoupling, interaction):
        rows, _, columns = amplitudes.shape
        own = amplitudes.reshape(rows, columns)
        weights = interaction.reshape(interaction.shape[0], interaction.shape[2])
        bounds = chunk_bounds(columns)
        lanes = max(width for _, width in bounds)
        entries = [(t, m) for t in span(reduce_bits) for m in (0, far, near, far ^ near)]
        matrix = recoupling.astype(F32)
        chain = Chain()
        tables, result, left, last_far = {}, None, None, None

        def table(transposed):
            if transposed not in tables:
                tables[transposed] = coefficients(chain, matrix.T if transposed else matrix, n_chan, entries, lanes)
            return tables[transposed]

        def mixing(block, transposed, note_far=None):
            other = swap(block, "chan", n_chan, far)
            beside = swap(block, "chan", n_chan, near)
            if note_far:
                note_far(other)
            yield "far"
            other, beside = chain.pin(other, beside)
            corner = swap(other, "chan", n_chan, near)
            held = [(0, block), (far, other), (near, beside), (far ^ near, corner)]
            targets, received = span(reduce_bits), []
            yield "near"
            for bit in reduce_bits:
                sent, targets = split(targets, bit)
                part = mix(chain, table(transposed), entries, held, sent, received)
                received.append((swap(part, "chan", n_chan, bit), [t ^ bit for t in sent]))
                yield "partial"
            return held, [r for r, _ in received]

        def one_chunk(lo, width):
            nonlocal result, left, last_far

            def note_far(array):
                nonlocal last_far
                last_far = array

            if left is None:
                block, left = mask_first(chain, block_rows, own, lo, width)
            else:
                block = mask_chunk(chain, left, own, lo, width, [last_far])
            held, received = yield from mixing(block, False, note_far)
            parts = mix_multiply(chain, table(False), entries, held, received, weights, n_row)
            got = [swap(parts[d], "row", n_row, d) for d in range(1, n_row)]
            yield "row"
            block = add_up(chain, [parts[0], *got])
            held, received = yield from mixing(block, True)
            result = finish(chain, table(True), entries, left, held, received, lo, columns, result)

        free = dict.fromkeys(LINK_SHARE, 0.0)
        queue, start = [], 0.0
        for i, (lo, width) in enumerate(bounds):
            queue.append((start, i, one_chunk(lo, width)))
            start += LINK_SHARE["far"] * width
        while queue:
            time, i, work = heapq.heappop(queue)
            kind = next(work, None)
            if kind is not None:
                free[kind] = max(time, free[kind]) + LINK_SHARE[kind] * bounds[i][1]
                heapq.heappush(queue, (free[kind] + LATENCY, i, work))
        return result.reshape(amplitudes.shape)

    return jax.shard_map(
        on_device,
        mesh=mesh,
        in_specs=(P("row", "chan", None), P("chan"), P(), P(None, "chan", "row")),
        out_specs=P("row", "chan", None),
        check_vma=False,
    )
```

```python
import functools
import heapq

import jax
import jax.numpy as jnp
from jax import lax
from jax.experimental import pallas as pl
from jax.experimental.pallas import tpu as pltpu
from jax.sharding import PartitionSpec as P

F32 = jnp.float32
BF16 = jnp.bfloat16
SLAB = 64
MATMUL_ROWS = 512
VMEM_LIMIT = 16 * 1024 * 1024
LINK_SHARE = {'far': 0.0311, 'near': 0.0421, 'partial': 0.0537, 'row': 0.0541}
LATENCY = 1.156

smem = pl.BlockSpec(memory_space=pltpu.SMEM)
vmem = pl.BlockSpec(memory_space=pltpu.VMEM)
unread = pl.BlockSpec(memory_space=pl.ANY)


def chunk_bounds(columns):
    if columns % 128:
        return [(0, columns)]
    units = columns // 128
    units = [2] + [1] * (units - 2) if units > 2 else [units]
    out, lo = [], 0
    for unit in units:
        out.append((lo, 128 * unit))
        lo += 128 * unit
    return out


class Chain:
    def call(self, kernel, name, out_shape, arrays, scalars=(), scratch=(), out_specs=None, whole=(), after=(), aliases=None):
        count = len(scalars) + len(arrays) + len(whole)
        outs = count + len(after)

        def body(*refs):
            kernel(*refs[:count], *refs[outs:outs + len(out_shape)], *refs[outs + len(out_shape):])

        return pl.pallas_call(
            body, name=name, out_shape=list(out_shape),
            in_specs=[smem] * len(scalars) + [vmem] * len(arrays) + [unread] * (outs - len(scalars) - len(arrays)),
            out_specs=out_specs or [vmem] * len(out_shape),
            scratch_shapes=list(scratch),
            input_output_aliases=aliases or {},
            compiler_params=pltpu.CompilerParams(vmem_limit_bytes=VMEM_LIMIT),
            cost_estimate=pl.CostEstimate(flops=0, transcendentals=0, bytes_accessed=sum(a.size * 2 for a in [*arrays, *out_shape])),
        )(*scalars, *arrays, *whole, *after)


def like(array):
    return jax.ShapeDtypeStruct(array.shape, array.dtype)


def slabs(rows, body, step=SLAB):
    step = step if rows % step == 0 else rows

    @pl.loop(0, rows // step)
    def _(i):
        body(pl.ds(pl.multiple_of(i * step, step), step))


def masked(total, at, left):
    row = lax.broadcasted_iota(jnp.int32, total.shape, 0) + at.start
    return jnp.where(row < left, total, 0.0).astype(BF16)


def stacked(count, rows, width):
    return jax.ShapeDtypeStruct((count, rows, width), BF16)


def mask_first(chain, block_rows, own, lo, width):
    rows = own.shape[0]

    def kernel(length_ref, own_ref, out_ref, left_ref, whole_ref):
        left = length_ref[0] - lax.axis_index("row") * rows
        left_ref[...] = jnp.full(left_ref.shape, left, jnp.int32)

        def body(at):
            kept = masked(own_ref[at, :].astype(F32), at, left)
            whole_ref[at, :] = kept
            out_ref[at, :] = kept[:, lo:lo + width]

        slabs(rows, body)

    outs = [jax.ShapeDtypeStruct((rows, width), BF16), jax.ShapeDtypeStruct((8, 256), jnp.int32), like(own)]
    return chain.call(kernel, "mask_first", outs, [own], [block_rows])


def mask_chunk(chain, left, own, lo, width, after):
    rows = own.shape[0]

    def kernel(left_ref, own_ref, out_ref):
        def body(at):
            out_ref[at, :] = masked(own_ref[at, lo:lo + width].astype(F32), at, left_ref[0:1, :width])

        slabs(rows, body)

    return chain.call(kernel, "mask_chunk", [jax.ShapeDtypeStruct((rows, width), BF16)], [left, own], after=after)[0]


def coefficients(chain, matrix, n_chan, entries, width):
    count = -(-len(entries) // 8) * 8

    def kernel(matrix_ref, in_ref, out_ref):
        c = lax.axis_index("chan")
        for i, (t, m) in enumerate(entries):
            in_ref[i:i + 1, :] = jnp.full((1, width), matrix_ref[c ^ t, c ^ m], F32)
            out_ref[i:i + 1, :] = jnp.full((1, width), matrix_ref[c ^ m, c ^ t], F32)

    return chain.call(kernel, "coefficients", [jax.ShapeDtypeStruct((count, width), F32)] * 2, [], [matrix])


def mixed(table_ref, entries, held, at, target):
    total = None
    for source, ref in held:
        entry = entries.index((target, source))
        term = ref[at, :] if not isinstance(ref, tuple) else ref[0][at, ref[1]:ref[1] + ref[2]]
        term = term.astype(F32) * table_ref[entry:entry + 1, :term.shape[1]]
        total = term if total is None else total + term
    return total


def mix(chain, table, entries, held, targets, received):
    rows, width = held[0][1].shape

    def kernel(table_ref, *refs):
        held_refs = [(m, (ref, b[1], width) if isinstance(b, tuple) else ref) for (m, b), ref in zip(held, refs)]
        received_refs = refs[len(held):-1]
        out_ref = refs[-1]

        def body(at):
            for i, t in enumerate(targets):
                total = mixed(table_ref, entries, held_refs, at, t)
                for (_, names), ref in zip(received, received_refs):
                    if t in names:
                        total = total + ref[names.index(t), at, :].astype(F32)
                out_ref[i, at, :] = total.astype(BF16)

        slabs(rows, body)

    arrays = [table] + [b[0] if isinstance(b, tuple) else b for _, b in held] + [r for r, _ in received]
    return chain.call(kernel, "mix", [stacked(len(targets), rows, width)], arrays)[0]


def mix_multiply(chain, table, entries, held, received, weights, n_row):
    rows, width = held[0][1].shape
    group = weights.shape[0] // n_row

    def kernel(table_ref, *refs):
        held_refs = [(m, (ref, b[1], width) if isinstance(b, tuple) else ref) for (m, b), ref in zip(held, refs)]
        received_refs = refs[len(held):len(held) + len(received)]
        weights_ref, *out_refs, cross_ref = refs[len(held) + len(received):]
        g = lax.axis_index("row")

        def body(at):
            total = mixed(table_ref, entries, held_refs, at, 0)
            for ref in received_refs:
                total = total + ref[0, at, :].astype(F32)
            cross_ref[at, :] = total.astype(BF16)

        slabs(rows, body)
        for d, out_ref in enumerate(out_refs):
            base = (g ^ d) * group

            def rows_of(at):
                from_row = pl.ds(pl.multiple_of(base + at.start, at.size), at.size)
                out_ref[at, :] = jnp.dot(weights_ref[from_row, :], cross_ref[...], preferred_element_type=F32).astype(BF16)

            slabs(group, rows_of, MATMUL_ROWS)

    arrays = [table] + [b[0] if isinstance(b, tuple) else b for _, b in held] + received + [weights]
    outs = [jax.ShapeDtypeStruct((group, width), BF16)] * n_row
    return chain.call(kernel, "mix_multiply", outs, arrays, scratch=[pltpu.VMEM((rows, width), BF16)])


def add_up(chain, blocks):
    def kernel(*refs):
        def body(at):
            terms = [ref[at, :].astype(F32) for ref in refs[:-1]]
            refs[-1][at, :] = functools.reduce(lambda a, b: a + b, terms).astype(BF16)

        slabs(blocks[0].shape[0], body)

    return chain.call(kernel, "add_up", [like(blocks[0])], blocks)[0]


def finish(chain, table, entries, left, held, received, lo, columns, result):
    rows, width = held[0][1].shape

    def kernel(table_ref, left_ref, *refs):
        held_refs = [(m, (ref, b[1], width) if isinstance(b, tuple) else ref) for (m, b), ref in zip(held, refs)]
        received_refs = refs[len(held):len(held) + len(received)]
        out_ref, chunk_ref, done = refs[-3:]

        def body(at):
            total = mixed(table_ref, entries, held_refs, at, 0)
            for ref in received_refs:
                total = total + ref[0, at, :].astype(F32)
            chunk_ref[at, :] = masked(total, at, left_ref[0:1, :width])

        slabs(rows, body)
        copy = pltpu.make_async_copy(chunk_ref, out_ref.at[:, lo:lo + width], done)
        copy.start()
        copy.wait()

    arrays = [table, left] + [b[0] if isinstance(b, tuple) else b for _, b in held] + received
    whole = [] if result is None else [result]
    return chain.call(
        kernel, "finish", [jax.ShapeDtypeStruct((rows, columns), BF16)], arrays,
        scratch=[pltpu.VMEM((rows, width), BF16), pltpu.SemaphoreType.DMA(())], out_specs=[unread],
        whole=whole, aliases={len(arrays): 0} if whole else {})[0]


def solution(mesh):
    n_chan, n_row = mesh.shape["chan"], mesh.shape["row"]
    chan_bits = [1 << b for b in range(n_chan.bit_length() - 1)]
    row_bits = [1 << b for b in range(n_row.bit_length() - 1)]
    far, near = chan_bits[-1], chan_bits[0]
    reduce_bits = [b for b in reversed(chan_bits) if b not in (far, near)]

    def swap(x, axis, size, bit):
        return lax.ppermute(x, axis, [(i, i ^ bit) for i in range(size)])

    def span(bits):
        targets = [0]
        for bit in bits:
            targets = targets + [t ^ bit for t in targets]
        return targets

    def split(targets, bit):
        return [t for t in targets if t & bit], [t for t in targets if not t & bit]

    def on_device(amplitudes, block_rows, recoupling, interaction):
        rows, _, columns = amplitudes.shape
        own = amplitudes.reshape(rows, columns)
        weights = interaction.reshape(interaction.shape[0], interaction.shape[2])
        bounds = chunk_bounds(columns)
        lanes = max(width for _, width in bounds)
        entries = [(t, m) for t in span(reduce_bits) for m in (0, far, near, far ^ near)]
        matrix = recoupling.astype(F32)
        chain = Chain()
        tables, result, left, last_far, whole_beside = [], None, None, None, None

        def table(transposed):
            if not tables:
                tables.extend(coefficients(chain, matrix, n_chan, entries, lanes))
            return tables[transposed]

        def mixing(block, transposed, beside=None):
            nonlocal last_far
            other = swap(block, "chan", n_chan, far)
            if transposed:
                beside = swap(block, "chan", n_chan, near)
            else:
                last_far = other
            yield "far"
            corner = swap(other, "chan", n_chan, near)
            held = [(0, block), (far, other), (near, beside), (far ^ near, corner)]
            targets, received = span(reduce_bits), []
            yield "near"
            for bit in reduce_bits:
                sent, targets = split(targets, bit)
                part = mix(chain, table(transposed), entries, held, sent, received)
                received.append((swap(part, "chan", n_chan, bit), [t ^ bit for t in sent]))
                yield "partial"
            return held, [r for r, _ in received]

        def one_chunk(lo, width):
            nonlocal result, left, whole_beside
            if left is None:
                block, left, whole_block = mask_first(chain, block_rows, own, lo, width)
                whole_beside = swap(whole_block, "chan", n_chan, near)
            else:
                block = mask_chunk(chain, left, own, lo, width, [last_far])
            held, received = yield from mixing(block, False, (whole_beside, lo))
            parts = mix_multiply(chain, table(False), entries, held, received, weights, n_row)
            got = [swap(parts[d], "row", n_row, d) for d in range(1, n_row)]
            yield "row"
            block = add_up(chain, [parts[0], *got])
            held, received = yield from mixing(block, True)
            result = finish(chain, table(True), entries, left, held, received, lo, columns, result)

        free = dict.fromkeys(LINK_SHARE, 0.0)
        queue, start = [], 0.0
        for i, (lo, width) in enumerate(bounds):
            queue.append((start, i, one_chunk(lo, width)))
            start += LINK_SHARE["far"] * width
        while queue:
            time, i, work = heapq.heappop(queue)
            kind = next(work, None)
            if kind is not None:
                free[kind] = max(time, free[kind]) + LINK_SHARE[kind] * bounds[i][1]
                heapq.heappush(queue, (free[kind] + LATENCY, i, work))
        return result.reshape(amplitudes.shape)

    return jax.shard_map(
        on_device,
        mesh=mesh,
        in_specs=(P("row", "chan", None), P("chan"), P(), P(None, "chan", "row")),
        out_specs=P("row", "chan", None),
        check_vma=False,
    )
```
